32 devices in a mesh: dp: 4 (over z), section: 4 (over x, core), et: 2 (over y).
Axes of the slice: x: 2, y: 2, z: 4, core: 2. Of those that a mesh axis runs over, the one named last changes fastest.
Arguments:
- handoff: bfloat16 [4, 1024, 3072], P('section', ('dp', 'et')), may hold values from -6 to 6
- fwd_slot: int32 [4, 1024], P('section', ('dp', 'et')), may hold values from -1 to 31, as said below
- fwd_weight: float32 [4, 1024], P('section', ('dp', 'et')), may hold values from 0.2 to 1
- stashed: bfloat16 [4, 1024, 3072], P('section', ('dp', 'et')), may hold values from -6 to 6
- back_slot: int32 [4, 1024], P('section', ('dp', 'et')), may hold values from -1 to 31, as said below
- back_weight: float32 [4, 1024], P('section', ('dp', 'et')), may hold values from 0.2 to 1
- grad_handoff: bfloat16 [4, 1024, 3072], P('section', ('dp', 'et')), may hold values from -6 to 6
- w_gate: bfloat16 [4, 3072, 5376], P('section', None, 'et'), may hold values from -0.109375 to 0.109375
- w_up: bfloat16 [4, 3072, 5376], P('section', None, 'et'), may hold values from -0.109375 to 0.109375
- w_down: bfloat16 [4, 5376, 3072], P('section', 'et'), may hold values from -0.078125 to 0.078125
Outputs:
- forward_out: bfloat16 [4, 1024, 3072], P('section', ('dp', 'et'))
- input_grad: bfloat16 [4, 1024, 3072], P('section', ('dp', 'et'))
- gate_grad: bfloat16 [4, 3072, 5376], P('section', 'dp', 'et')
- up_grad: bfloat16 [4, 3072, 5376], P('section', 'dp', 'et')
- down_grad: bfloat16 [4, 5376, 3072], P('section', 'et', 'dp')
The draws below stay inside these ranges and needn't reach their ends.
Inputs may be any that keep to these rules, and one draw needn't show every extreme that they name: `fwd_slot`: within each group of 128 rows of one device, the tokens routed to the expert carry the slots 0, 1, 2, ... in the order of the rows and the others carry -1; at least a quarter of 32 are routed; some device has exactly 32 routed tokens. `back_slot`: as for fwd_slot.
All inputs are finite; a program needn't handle non-finite values.
Results may differ from the reference program's by a relative error of at most 0.02.
Values may be sent and summed in bfloat16 or wider, within the bound.
A program may use at most 192 MiB of HBM per device.

```python
import jax
import jax.numpy as jnp
from jax import lax

D = 3072
FF_WIN = 5376
TOK_DEV = 128
CAP = 32
TOKENS = 1024
SECTIONS = 4
N_DP = 4
N_ET = 2


def route_slots(key):
    blocks = TOKENS // TOK_DEV * SECTIONS
    key_order, key_count, key_full = jax.random.split(key, 3)
    scores = jax.random.randint(key_order, (blocks, TOK_DEV), 0, 2 ** 20)
    scores = scores * TOK_DEV + lax.broadcasted_iota(jnp.int32, (blocks, TOK_DEV), 1)
    ordering = jnp.argsort(jnp.argsort(scores, axis=1), axis=1).astype(jnp.int32)
    counts = jax.random.randint(key_count, (blocks,), CAP // 4, CAP + 1)
    fullest = jax.random.randint(key_full, (), 0, blocks)
    counts = jnp.where(jnp.arange(blocks) == fullest, CAP, counts)
    chosen = (ordering < counts[:, None]).astype(jnp.int32)
    slot_ids = jnp.where(chosen > 0, jnp.cumsum(chosen, axis=1) - 1, -1)
    return slot_ids.reshape(SECTIONS, TOKENS).astype(jnp.int32)


def draw_fwd_slot(key, part):
    key = jax.random.fold_in(key, 11)
    return route_slots(key)


def draw_back_slot(key, part):
    key = jax.random.fold_in(key, 23)
    return route_slots(key)


def level_of(stream_key, extent, shards, low, largest):
    def one(position, parts):
        steps = jax.random.uniform(jax.random.fold_in(jax.random.fold_in(stream_key, 6), position), (parts,), jnp.float32, low / len(shards), largest / len(shards))
        return jnp.repeat(jnp.exp(steps), extent[position] // parts).reshape((-1,) + (1,) * (len(extent) - position - 1))

    level = one(*shards[0])
    for cut in shards[1:]:
        level = level * one(*cut)
    return level


def normal_values(rng, shape, spread, reach, cuts=(), kind=jnp.bfloat16):
    array = spread * jax.random.normal(rng, shape, jnp.float32)
    if cuts:
        array = array * level_of(rng, shape, cuts, -0.22, 0.18)
    return jnp.clip(array, -reach, reach).astype(kind)


def setup_inputs(seed: int = 0) -> dict:
    keys = jax.random.split(jax.random.key(seed), 11)
    return {
        "handoff": normal_values(keys[0], (SECTIONS, TOKENS, D), 1.0, 6.0, ((0, 4), (1, 8))),
        "fwd_slot": draw_fwd_slot(jax.random.fold_in(keys[10], 71), 0),
        "fwd_weight": jnp.clip(0.2 + 0.8 * jax.random.uniform(keys[2], (SECTIONS, TOKENS), jnp.float32) ** level_of(keys[2], (SECTIONS, TOKENS), ((0, 4), (1, 8)), -0.2, 0.2), 0.2, 1.0),
        "stashed": normal_values(keys[3], (SECTIONS, TOKENS, D), 1.0, 6.0, ((0, 4), (1, 8))),
        "back_slot": draw_back_slot(jax.random.fold_in(keys[10], 71), 0),
        "back_weight": jnp.clip(0.2 + 0.8 * jax.random.uniform(keys[5], (SECTIONS, TOKENS), jnp.float32) ** level_of(keys[5], (SECTIONS, TOKENS), ((0, 4), (1, 8)), -0.2, 0.2), 0.2, 1.0),
        "grad_handoff": normal_values(keys[6], (SECTIONS, TOKENS, D), 1.0, 6.0, ((0, 4), (1, 8))),
        "w_gate": normal_values(keys[7], (SECTIONS, D, FF_WIN), D ** -0.5, 0.109375, ((0, 4), (2, 2))),
        "w_up": normal_values(keys[8], (SECTIONS, D, FF_WIN), D ** -0.5, 0.109375, ((0, 4), (2, 2))),
        "w_down": normal_values(keys[9], (SECTIONS, FF_WIN, D), FF_WIN ** -0.5, 0.078125, ((0, 4), (1, 2))),
    }


def rounded(value):
    return lax.optimization_barrier(value.astype(jnp.bfloat16)).astype(jnp.float32)


def pack_replica(row_block, slot_ids):
    sources = jnp.arange(N_ET * TOK_DEV, dtype=jnp.int32) // TOK_DEV
    target = jnp.where(slot_ids >= 0, sources * CAP + slot_ids, N_ET * CAP).astype(jnp.int32)
    packed = jnp.zeros((N_ET * CAP, row_block.shape[1]), row_block.dtype)
    return packed.at[target].set(row_block, mode="drop"), target


def unpack_replica(summed, target, slot_ids):
    picked = jnp.take(summed, jnp.minimum(target, N_ET * CAP - 1), axis=0)
    return jnp.where(slot_ids[:, None] >= 0, picked, jnp.zeros_like(picked))


def column_sum(make_term):
    share_cols = FF_WIN // N_ET
    summed = None
    for member in range(N_ET):
        partial_value = rounded(make_term(slice(member * share_cols, (member + 1) * share_cols)))
        summed = partial_value if summed is None else summed + partial_value
    return summed


def activations(packed, gate_w, up_w):
    pre_gate = jnp.dot(packed, gate_w, preferred_element_type=jnp.float32)
    pre_up = jnp.dot(packed, up_w, preferred_element_type=jnp.float32)
    sigmoid_gate = jax.nn.sigmoid(pre_gate)
    active = pre_gate * sigmoid_gate
    hidden = (active * pre_up).astype(jnp.bfloat16)
    return pre_gate, pre_up, sigmoid_gate, active, hidden


def reference(handoff, fwd_slot, fwd_weight, stashed, back_slot, back_weight, grad_handoff, w_gate, w_up, w_down):
    replica_rows = N_ET * TOK_DEV
    forward_list, input_list = [], []
    gate_list, up_list, down_list = [], [], []
    for section_id in range(SECTIONS):
        arrived = handoff[(section_id - 1) % SECTIONS]
        returned = grad_handoff[(section_id + 1) % SECTIONS]
        gate_w, up_w, down_w = w_gate[section_id], w_up[section_id], w_down[section_id]
        forward_rows, input_rows = [], []
        gate_acc = jnp.zeros((D, FF_WIN), jnp.float32)
        up_acc = jnp.zeros((D, FF_WIN), jnp.float32)
        down_acc = jnp.zeros((FF_WIN, D), jnp.float32)
        for replica in range(N_DP):
            first_row = replica * replica_rows
            last_row = first_row + replica_rows
            slot_ids = fwd_slot[section_id, first_row:last_row]
            packed, target = pack_replica(arrived[first_row:last_row], slot_ids)
            hidden = activations(packed, gate_w, up_w)[4]
            summed = column_sum(lambda columns: jnp.dot(hidden[:, columns], down_w[columns], preferred_element_type=jnp.float32))
            weights_row = fwd_weight[section_id, first_row:last_row]
            forward_rows.append((weights_row[:, None] * unpack_replica(summed, target, slot_ids)).astype(jnp.bfloat16))

            back_ids = back_slot[section_id, first_row:last_row]
            scaled = (back_weight[section_id, first_row:last_row][:, None] * returned[first_row:last_row].astype(jnp.float32)).astype(jnp.bfloat16)
            packed_grad, back_target = pack_replica(scaled, back_ids)
            packed_back, _ = pack_replica(stashed[section_id, first_row:last_row], back_ids)
            pre_gate, pre_up, sigmoid_gate, active, hidden = activations(packed_back, gate_w, up_w)
            grad_hidden = jnp.dot(packed_grad, down_w.T, preferred_element_type=jnp.float32)
            grad_upact = (grad_hidden * active).astype(jnp.bfloat16)
            grad_gateact = (grad_hidden * pre_up * sigmoid_gate * (1.0 + pre_gate * (1.0 - sigmoid_gate))).astype(jnp.bfloat16)
            gate_acc = gate_acc + rounded(jnp.dot(packed_back.T, grad_gateact, preferred_element_type=jnp.float32))
            up_acc = up_acc + rounded(jnp.dot(packed_back.T, grad_upact, preferred_element_type=jnp.float32))
            down_acc = down_acc + rounded(jnp.dot(hidden.T, packed_grad, preferred_element_type=jnp.float32))
            grad_packed = column_sum(lambda columns: jnp.dot(grad_gateact[:, columns], gate_w[:, columns].T, preferred_element_type=jnp.float32) + jnp.dot(grad_upact[:, columns], up_w[:, columns].T, preferred_element_type=jnp.float32))
            input_rows.append(unpack_replica(grad_packed, back_target, back_ids).astype(jnp.bfloat16))
        forward_list.append(jnp.concatenate(forward_rows, axis=0))
        input_list.append(jnp.concatenate(input_rows, axis=0))
        gate_list.append(gate_acc.astype(jnp.bfloat16))
        up_list.append(up_acc.astype(jnp.bfloat16))
        down_list.append(down_acc.astype(jnp.bfloat16))
    return (jnp.stack(forward_list), jnp.stack(input_list), jnp.stack(gate_list), jnp.stack(up_list), jnp.stack(down_list))
```

```python
import functools

import jax
import jax.numpy as jnp
from jax import lax
from jax.experimental import pallas as pl
from jax.experimental.pallas import tpu as pltpu
from jax.sharding import PartitionSpec as P

CAP = 32
NN = (((1,), (0,)), ((), ()))
NT = (((1,), (1,)), ((), ()))
TN = (((0,), (0,)), ((), ()))


def mul(a, b, dims=NN):
    return lax.dot_general(a, b, dims, preferred_element_type=jnp.float32)


def passed_along(block, axis, distance):
    n = lax.axis_size(axis)
    return lax.ppermute(block, axis, [((i - distance) % n, i) for i in range(n)])


def pack_rows(row_block, slot_ids):
    places = lax.broadcasted_iota(jnp.int32, (CAP, slot_ids.shape[0]), 0)
    picker = (places == slot_ids[None, :]).astype(jnp.bfloat16)
    return mul(picker, row_block).astype(jnp.bfloat16)


def pack_values(values, slot_ids):
    places = lax.broadcasted_iota(jnp.int32, (CAP, slot_ids.shape[0]), 0)
    return jnp.sum(jnp.where(places == slot_ids[None, :], values[None, :], 0.0), axis=1)


def unpack_rows(packed, slot_ids):
    places = lax.broadcasted_iota(jnp.int32, (slot_ids.shape[0], CAP), 1)
    picker = (places == slot_ids[:, None]).astype(jnp.float32)
    return jnp.dot(
        picker, packed, precision=lax.Precision.HIGHEST, preferred_element_type=jnp.float32
    )


def gather_et(rows):
    if lax.axis_size("et") == 2:
        return jnp.concatenate([rows, passed_along(rows, "et", 1)], axis=0)
    return lax.all_gather(rows, "et", axis=0, tiled=True)


def scatter_et(partial):
    if lax.axis_size("et") == 2:
        other = passed_along(partial[CAP:], "et", 1)
        return partial[:CAP].astype(jnp.float32) + other.astype(jnp.float32)
    return lax.psum_scatter(partial, "et", scatter_dimension=0, tiled=True).astype(jnp.float32)


def gates(pre_gate, pre_up, grad_hidden):
    sig = jax.nn.sigmoid(pre_gate)
    active = pre_gate * sig
    hidden = (active * pre_up).astype(jnp.bfloat16)
    grad_up = (grad_hidden * active).astype(jnp.bfloat16)
    grad_gate = (grad_hidden * pre_up * sig * (1.0 + pre_gate * (1.0 - sig))).astype(jnp.bfloat16)
    return hidden, grad_gate, grad_up


def back_kernel(
    own_rows,
    back_ref,
    grad_ref,
    back_cols_t,
    grad_cols,
    gate_ref,
    up_ref,
    down_ref,
    gate_out,
    up_out,
    down_out,
    rows_out,
    gate_act,
    up_act,
    total,
):
    step = pl.program_id(0)
    pre_gate = mul(back_ref[...], gate_ref[...])
    pre_up = mul(back_ref[...], up_ref[...])
    grad_hidden = mul(grad_ref[...], down_ref[...], NT)
    hidden, grad_gate, grad_up = gates(pre_gate, pre_up, grad_hidden)
    gate_act[...] = grad_gate
    up_act[...] = grad_up
    gate_out[...] = mul(back_cols_t[...], grad_gate).astype(jnp.bfloat16)
    up_out[...] = mul(back_cols_t[...], grad_up).astype(jnp.bfloat16)
    down_out[...] = mul(hidden, grad_cols[...], TN).astype(jnp.bfloat16)
    own = pl.ds(pl.multiple_of(lax.axis_index("dp") * own_rows, own_rows), own_rows)
    term = mul(gate_act[own, :], gate_ref[...], NT) + mul(up_act[own, :], up_ref[...], NT)

    @pl.when(step == 0)
    def _():
        total[...] = term

    @pl.when(step > 0)
    def _():
        total[...] += term

    @pl.when(step == pl.num_programs(0) - 1)
    def _():
        rows_out[...] = total[...].astype(jnp.bfloat16)


def backward(back_all, grad_all, back_cols, grad_cols, gate_w, up_w, down_w, tile):
    rows, depth = back_all.shape
    share = back_cols.shape[1]
    units = gate_w.shape[1]
    own_rows = rows // lax.axis_size("dp")
    whole = lambda i: (0, 0)
    once = functools.partial(pl.BlockSpec, index_map=whole, pipeline_mode=pl.Buffered(1))
    across = lambda i: (0, i)
    down = lambda i: (i, 0)
    flops = 2 * units * (3 * rows * depth + 2 * own_rows * depth + 3 * rows * share)
    return pl.pallas_call(
        functools.partial(back_kernel, own_rows),
        grid=(units // tile,),
        in_specs=[
            once((rows, depth)),
            once((rows, depth)),
            once((share, rows)),
            once((rows, share)),
            pl.BlockSpec((depth, tile), across),
            pl.BlockSpec((depth, tile), across),
            pl.BlockSpec((tile, depth), down),
        ],
        out_specs=[
            pl.BlockSpec((share, tile), across),
            pl.BlockSpec((share, tile), across),
            pl.BlockSpec((tile, share), down),
            pl.BlockSpec((own_rows, depth), whole),
        ],
        out_shape=[
            jax.ShapeDtypeStruct((share, units), jnp.bfloat16),
            jax.ShapeDtypeStruct((share, units), jnp.bfloat16),
            jax.ShapeDtypeStruct((units, share), jnp.bfloat16),
            jax.ShapeDtypeStruct((own_rows, depth), jnp.bfloat16),
        ],
        scratch_shapes=[
            pltpu.VMEM((rows, tile), jnp.bfloat16),
            pltpu.VMEM((rows, tile), jnp.bfloat16),
            pltpu.VMEM((own_rows, depth), jnp.float32),
        ],
        compiler_params=pltpu.CompilerParams(vmem_limit_bytes=48 * 2**20),
        cost_estimate=pl.CostEstimate(
            flops=flops,
            bytes_accessed=6 * units * (depth + share) + 8 * rows * depth,
            transcendentals=rows * units,
        ),
    )(back_all, grad_all, back_cols.T, grad_cols, gate_w, up_w, down_w)


def backward_plain(back_all, grad_all, back_cols, grad_cols, gate_w, up_w, down_w):
    pre_gate, pre_up = mul(back_all, gate_w), mul(back_all, up_w)
    hidden, grad_gate, grad_up = gates(pre_gate, pre_up, mul(grad_all, down_w, NT))
    own_rows = back_all.shape[0] // lax.axis_size("dp")
    start = lax.axis_index("dp") * own_rows
    own_gate = lax.dynamic_slice_in_dim(grad_gate, start, own_rows, 0)
    own_up = lax.dynamic_slice_in_dim(grad_up, start, own_rows, 0)
    return (
        mul(back_cols, grad_gate, TN).astype(jnp.bfloat16),
        mul(back_cols, grad_up, TN).astype(jnp.bfloat16),
        mul(hidden, grad_cols, TN).astype(jnp.bfloat16),
        (mul(own_gate, gate_w, NT) + mul(own_up, up_w, NT)).astype(jnp.bfloat16),
    )


def per_device(
    handoff,
    fwd_slot,
    fwd_weight,
    stashed,
    back_slot,
    back_weight,
    grad_handoff,
    w_gate,
    w_up,
    w_down,
):
    gate_w, up_w, down_w = (w_gate[0], w_up[0], w_down[0])
    fwd_ids, back_ids = fwd_slot[0], back_slot[0]
    back_ids_there = passed_along(back_slot, "section", 1)[0]
    fwd_ids_there = passed_along(fwd_slot, "section", -1)[0]
    stash_packed = pack_rows(stashed[0], back_ids)
    back_all = lax.all_gather(stash_packed, ("dp", "et"), axis=0, tiled=True)
    returned = passed_along(pack_rows(grad_handoff[0], back_ids_there), "section", -1)
    weights = pack_values(back_weight[0], back_ids)
    grad_packed = (weights[:, None] * returned.astype(jnp.float32)).astype(jnp.bfloat16)
    grad_all = lax.all_gather(grad_packed, ("dp", "et"), axis=0, tiled=True)

    arrived = passed_along(pack_rows(handoff[0], fwd_ids_there), "section", 1)
    fwd_rows = gather_et(arrived)
    pre_gate = mul(fwd_rows, gate_w)
    pre_up = mul(fwd_rows, up_w)
    hidden = (pre_gate * jax.nn.sigmoid(pre_gate) * pre_up).astype(jnp.bfloat16)
    own_sum = scatter_et(mul(hidden, down_w).astype(jnp.bfloat16))
    forward_out = (fwd_weight[0][:, None] * unpack_rows(own_sum, fwd_ids)).astype(jnp.bfloat16)

    share = gate_w.shape[0] // lax.axis_size("dp")
    first = lax.axis_index("dp") * share
    back_cols = lax.dynamic_slice_in_dim(back_all, first, share, 1)
    grad_cols = lax.dynamic_slice_in_dim(grad_all, first, share, 1)
    operands = (back_all, grad_all, back_cols, grad_cols, gate_w, up_w, down_w)
    tiles = [t for t in (384, 256, 128) if gate_w.shape[1] % t == 0]
    if tiles and back_all.shape[0] <= 512:
        gate_sum, up_sum, down_sum, partial = backward(*operands, tiles[0])
    else:
        gate_sum, up_sum, down_sum, partial = backward_plain(*operands)
    if lax.axis_size("et") == 2:
        partial = jnp.where(
            lax.axis_index("et") == 0, partial, jnp.concatenate([partial[CAP:], partial[:CAP]])
        )
    grad_rows = unpack_rows(scatter_et(partial), back_ids).astype(jnp.bfloat16)
    return (
        forward_out[None],
        grad_rows[None],
        gate_sum[None],
        up_sum[None],
        down_sum[None],
    )


def solution(mesh):
    rows3 = P("section", ("dp", "et"), None)
    rows2 = P("section", ("dp", "et"))
    columns = P("section", None, "et")
    return jax.shard_map(
        per_device,
        mesh=mesh,
        in_specs=(
            rows3, rows2, rows2, rows3, rows2, rows2, rows3,
            columns, columns, P("section", "et", None),
        ),
        out_specs=(
            rows3,
            rows3,
            P("section", "dp", "et"),
            P("section", "dp", "et"),
            P("section", "et", "dp"),
        ),
        check_vma=False,
    )
```

```python
import functools

import jax
import jax.numpy as jnp
from jax import lax
from jax.experimental import pallas as pl
from jax.experimental.pallas import tpu as pltpu
from jax.sharding import PartitionSpec as P

CAP = 32
NN = (((1,), (0,)), ((), ()))
NT = (((1,), (1,)), ((), ()))
TN = (((0,), (0,)), ((), ()))


def mul(a, b, dims=NN):
    return lax.dot_general(a, b, dims, preferred_element_type=jnp.float32)


def passed_along(block, axis, distance):
    n = lax.axis_size(axis)
    return lax.ppermute(block, axis, [((i - distance) % n, i) for i in range(n)])


def pack_rows(row_block, slot_ids):
    places = lax.broadcasted_iota(jnp.int32, (CAP, slot_ids.shape[0]), 0)
    picker = (places == slot_ids[None, :]).astype(jnp.bfloat16)
    return mul(picker, row_block).astype(jnp.bfloat16)


def pack_values(values, slot_ids):
    places = lax.broadcasted_iota(jnp.int32, (CAP, slot_ids.shape[0]), 0)
    return jnp.sum(jnp.where(places == slot_ids[None, :], values[None, :], 0.0), axis=1)


def unpack_rows(packed, slot_ids):
    places = lax.broadcasted_iota(jnp.int32, (slot_ids.shape[0], CAP), 1)
    picker = (places == slot_ids[:, None]).astype(jnp.float32)
    return jnp.dot(
        picker, packed, precision=lax.Precision.HIGHEST, preferred_element_type=jnp.float32
    )


def gather_et(rows):
    if lax.axis_size("et") == 2:
        return jnp.concatenate([rows, passed_along(rows, "et", 1)], axis=0)
    return lax.all_gather(rows, "et", axis=0, tiled=True)


def scatter_et(partial):
    if lax.axis_size("et") == 2:
        other = passed_along(partial[CAP:], "et", 1)
        return partial[:CAP].astype(jnp.float32) + other.astype(jnp.float32)
    return lax.psum_scatter(partial, "et", scatter_dimension=0, tiled=True).astype(jnp.float32)


def gather_replicas(rows):
    if lax.axis_size("et") == 2:
        blocks = [rows] + [passed_along(rows, "dp", d) for d in range(1, lax.axis_size("dp"))]
        pairs = [piece for block in blocks for piece in (block, passed_along(block, "et", 1))]
        return pairs, 0
    own = lax.axis_index("dp") * lax.axis_size("et") * rows.shape[0]
    return [lax.all_gather(rows, ("dp", "et"), axis=0, tiled=True)], own


def gates(pre_gate, pre_up, grad_hidden):
    sig = jax.nn.sigmoid(pre_gate)
    active = pre_gate * sig
    hidden = (active * pre_up).astype(jnp.bfloat16)
    grad_up = (grad_hidden * active).astype(jnp.bfloat16)
    grad_gate = (grad_hidden * pre_up * sig * (1.0 + pre_gate * (1.0 - sig))).astype(jnp.bfloat16)
    return hidden, grad_gate, grad_up


def back_kernel(
    own_rows,
    back_ref,
    grad_ref,
    back_cols,
    grad_cols,
    gate_ref,
    up_ref,
    down_ref,
    gate_out,
    up_out,
    down_out,
    rows_out,
    total,
    back_cols_t,
):
    step = pl.program_id(0)

    @pl.when(step == 0)
    def _():
        back_cols_t[...] = back_cols[...].T

    pre_gate = mul(back_ref[...], gate_ref[...])
    pre_up = mul(back_ref[...], up_ref[...])
    grad_hidden = mul(grad_ref[...], down_ref[...], NT)
    hidden, grad_gate, grad_up = gates(pre_gate, pre_up, grad_hidden)
    gate_out[...] = mul(back_cols_t[...], grad_gate).astype(jnp.bfloat16)
    up_out[...] = mul(back_cols_t[...], grad_up).astype(jnp.bfloat16)
    down_out[...] = mul(hidden, grad_cols[...], TN).astype(jnp.bfloat16)
    term = mul(grad_gate[:own_rows], gate_ref[...], NT)
    term += mul(grad_up[:own_rows], up_ref[...], NT)

    @pl.when(step == 0)
    def _():
        total[...] = term

    @pl.when(step > 0)
    def _():
        total[...] += term

    @pl.when(step == pl.num_programs(0) - 1)
    def _():
        rows_out[...] = total[...].astype(jnp.bfloat16)


def backward(back_all, grad_all, back_cols, grad_cols, gate_w, up_w, down_w, tile):
    rows, depth = back_all.shape
    share = back_cols.shape[1]
    units = gate_w.shape[1]
    own_rows = rows // lax.axis_size("dp")
    whole = lambda i: (0, 0)
    once = functools.partial(pl.BlockSpec, index_map=whole, pipeline_mode=pl.Buffered(1))
    across = lambda i: (0, i)
    down = lambda i: (i, 0)
    flops = 2 * units * (3 * rows * depth + 2 * own_rows * depth + 3 * rows * share)
    return pl.pallas_call(
        functools.partial(back_kernel, own_rows),
        grid=(units // tile,),
        in_specs=[
            once((rows, depth)),
            once((rows, depth)),
            once((rows, share)),
            once((rows, share)),
            pl.BlockSpec((depth, tile), across),
            pl.BlockSpec((depth, tile), across),
            pl.BlockSpec((tile, depth), down),
        ],
        out_specs=[
            pl.BlockSpec((share, tile), across),
            pl.BlockSpec((share, tile), across),
            pl.BlockSpec((tile, share), down),
            pl.BlockSpec((own_rows, depth), whole),
        ],
        out_shape=[
            jax.ShapeDtypeStruct((share, units), jnp.bfloat16),
            jax.ShapeDtypeStruct((share, units), jnp.bfloat16),
            jax.ShapeDtypeStruct((units, share), jnp.bfloat16),
            jax.ShapeDtypeStruct((own_rows, depth), jnp.bfloat16),
        ],
        scratch_shapes=[
            pltpu.VMEM((own_rows, depth), jnp.float32),
            pltpu.VMEM((share, rows), jnp.bfloat16),
        ],
        compiler_params=pltpu.CompilerParams(vmem_limit_bytes=48 * 2**20),
        cost_estimate=pl.CostEstimate(
            flops=flops,
            bytes_accessed=6 * units * (depth + share) + 8 * rows * depth,
            transcendentals=rows * units,
        ),
    )(back_all, grad_all, back_cols, grad_cols, gate_w, up_w, down_w)


def backward_plain(back_all, grad_all, back_cols, grad_cols, gate_w, up_w, down_w, start):
    pre_gate, pre_up = mul(back_all, gate_w), mul(back_all, up_w)
    hidden, grad_gate, grad_up = gates(pre_gate, pre_up, mul(grad_all, down_w, NT))
    own_rows = back_all.shape[0] // lax.axis_size("dp")
    own_gate = lax.dynamic_slice_in_dim(grad_gate, start, own_rows, 0)
    own_up = lax.dynamic_slice_in_dim(grad_up, start, own_rows, 0)
    return (
        mul(back_cols, grad_gate, TN).astype(jnp.bfloat16),
        mul(back_cols, grad_up, TN).astype(jnp.bfloat16),
        mul(hidden, grad_cols, TN).astype(jnp.bfloat16),
        (mul(own_gate, gate_w, NT) + mul(own_up, up_w, NT)).astype(jnp.bfloat16),
    )


def per_device(
    handoff,
    fwd_slot,
    fwd_weight,
    stashed,
    back_slot,
    back_weight,
    grad_handoff,
    w_gate,
    w_up,
    w_down,
):
    gate_w, up_w, down_w = (w_gate[0], w_up[0], w_down[0])
    fwd_ids, back_ids = fwd_slot[0], back_slot[0]
    back_ids_there = passed_along(back_slot, "section", 1)[0]
    fwd_ids_there = passed_along(fwd_slot, "section", -1)[0]
    stash_packed = pack_rows(stashed[0], back_ids)
    back_pieces, own = gather_replicas(stash_packed)
    returned = passed_along(pack_rows(grad_handoff[0], back_ids_there), "section", -1)
    weights = pack_values(back_weight[0], back_ids)
    grad_packed = (weights[:, None] * returned.astype(jnp.float32)).astype(jnp.bfloat16)
    grad_pieces = gather_replicas(grad_packed)[0]

    arrived = passed_along(pack_rows(handoff[0], fwd_ids_there), "section", 1)
    fwd_rows = gather_et(arrived)
    pre_gate = mul(fwd_rows, gate_w)
    pre_up = mul(fwd_rows, up_w)
    hidden = (pre_gate * jax.nn.sigmoid(pre_gate) * pre_up).astype(jnp.bfloat16)
    fwd_partial = mul(hidden, down_w).astype(jnp.bfloat16)
    fwd_partial, back_pieces, grad_pieces = lax.optimization_barrier(
        (fwd_partial, back_pieces, grad_pieces)
    )
    own_sum = scatter_et(fwd_partial)
    forward_out = (fwd_weight[0][:, None] * unpack_rows(own_sum, fwd_ids)).astype(jnp.bfloat16)

    back_all = jnp.concatenate(back_pieces, axis=0)
    grad_all = jnp.concatenate(grad_pieces, axis=0)
    share = gate_w.shape[0] // lax.axis_size("dp")
    first = lax.axis_index("dp") * share
    back_cols = lax.dynamic_slice_in_dim(back_all, first, share, 1)
    grad_cols = lax.dynamic_slice_in_dim(grad_all, first, share, 1)
    operands = (back_all, grad_all, back_cols, grad_cols, gate_w, up_w, down_w)
    tiles = [t for t in (384, 256, 128) if gate_w.shape[1] % t == 0]
    if tiles and lax.axis_size("et") == 2 and back_all.shape[0] <= 512:
        gate_sum, up_sum, down_sum, partial = backward(*operands, tiles[0])
    else:
        gate_sum, up_sum, down_sum, partial = backward_plain(*operands, own)
    grad_rows = unpack_rows(scatter_et(partial), back_ids).astype(jnp.bfloat16)
    return (
        forward_out[None],
        grad_rows[None],
        gate_sum[None],
        up_sum[None],
        down_sum[None],
    )


def solution(mesh):
    rows3 = P("section", ("dp", "et"), None)
    rows2 = P("section", ("dp", "et"))
    columns = P("section", None, "et")
    return jax.shard_map(
        per_device,
        mesh=mesh,
        in_specs=(
            rows3, rows2, rows2, rows3, rows2, rows2, rows3,
            columns, columns, P("section", "et", None),
        ),
        out_specs=(
            rows3,
            rows3,
            P("section", "dp", "et"),
            P("section", "dp", "et"),
            P("section", "et", "dp"),
        ),
        check_vma=False,
    )
```

```python
import functools

import jax
import jax.numpy as jnp
from jax import lax
from jax.experimental import pallas as pl
from jax.experimental.pallas import tpu as pltpu
from jax.sharding import PartitionSpec as P

CAP = 32
NN = (((1,), (0,)), ((), ()))
NT = (((1,), (1,)), ((), ()))
TN = (((0,), (0,)), ((), ()))


def mul(a, b, dims=NN):
    return lax.dot_general(a, b, dims, preferred_element_type=jnp.float32)


def passed_along(block, axis, distance):
    n = lax.axis_size(axis)
    return lax.ppermute(block, axis, [((i - distance) % n, i) for i in range(n)])


def pack_rows(row_block, slot_ids):
    places = lax.broadcasted_iota(jnp.int32, (CAP, slot_ids.shape[0]), 0)
    picker = (places == slot_ids[None, :]).astype(jnp.bfloat16)
    return mul(picker, row_block).astype(jnp.bfloat16)


def pack_values(values, slot_ids):
    places = lax.broadcasted_iota(jnp.int32, (CAP, slot_ids.shape[0]), 0)
    return jnp.sum(jnp.where(places == slot_ids[None, :], values[None, :], 0.0), axis=1)


def unpack_rows(packed, slot_ids):
    places = lax.broadcasted_iota(jnp.int32, (slot_ids.shape[0], CAP), 1)
    picker = (places == slot_ids[:, None]).astype(jnp.float32)
    return jnp.dot(
        picker, packed, precision=lax.Precision.HIGHEST, preferred_element_type=jnp.float32
    )


def gather_et(rows):
    if lax.axis_size("et") == 2:
        return jnp.concatenate([rows, passed_along(rows, "et", 1)], axis=0)
    return lax.all_gather(rows, "et", axis=0, tiled=True)


def sent_part(partial):
    if lax.axis_size("et") == 2:
        return passed_along(partial[CAP:], "et", 1).astype(jnp.float32)
    return lax.psum_scatter(partial, "et", scatter_dimension=0, tiled=True).astype(jnp.float32)


def with_own(partial, sent):
    if lax.axis_size("et") == 2:
        return partial[:CAP].astype(jnp.float32) + sent
    return sent


def gates(pre_gate, pre_up, grad_hidden):
    sig = jax.nn.sigmoid(pre_gate)
    active = pre_gate * sig
    hidden = (active * pre_up).astype(jnp.bfloat16)
    grad_up = (grad_hidden * active).astype(jnp.bfloat16)
    grad_gate = (grad_hidden * pre_up * sig * (1.0 + pre_gate * (1.0 - sig))).astype(jnp.bfloat16)
    return hidden, grad_gate, grad_up


def back_kernel(own_rows, n_pieces, *refs):
    pieces, refs = refs[:n_pieces], refs[n_pieces:]
    gate_ref, up_ref, down_ref, gate_out, up_out, down_out, rows_out = refs[:7]
    back_ref, grad_ref, back_cols_t, grad_cols, total = refs[7:]
    step = pl.program_id(0)
    share = grad_cols.shape[1]

    @pl.when(step == 0)
    def _():
        for k, piece in enumerate(pieces):
            back_ref[k * CAP : (k + 1) * CAP] = piece[:CAP]
            grad_ref[k * CAP : (k + 1) * CAP] = piece[CAP:]
        columns = pl.ds(pl.multiple_of(lax.axis_index("dp") * share, 128), share)
        back_cols_t[...] = back_ref[:, columns].T
        grad_cols[...] = grad_ref[:, columns]

    pre_gate = mul(back_ref[...], gate_ref[...])
    pre_up = mul(back_ref[...], up_ref[...])
    grad_hidden = mul(grad_ref[...], down_ref[...], NT)
    hidden, grad_gate, grad_up = gates(pre_gate, pre_up, grad_hidden)
    gate_out[...] = mul(back_cols_t[...], grad_gate).astype(jnp.bfloat16)
    up_out[...] = mul(back_cols_t[...], grad_up).astype(jnp.bfloat16)
    down_out[...] = mul(hidden, grad_cols[...], TN).astype(jnp.bfloat16)
    term = mul(grad_gate[:own_rows], gate_ref[...], NT)
    term += mul(grad_up[:own_rows], up_ref[...], NT)

    @pl.when(step == 0)
    def _():
        total[...] = term

    @pl.when(step > 0)
    def _():
        total[...] += term

    @pl.when(step == pl.num_programs(0) - 1)
    def _():
        rows_out[...] = total[...].astype(jnp.bfloat16)


def backward(pieces, gate_w, up_w, down_w, tile):
    rows, depth = len(pieces) * CAP, gate_w.shape[0]
    share = depth // lax.axis_size("dp")
    units = gate_w.shape[1]
    own_rows = rows // lax.axis_size("dp")
    whole = lambda i: (0, 0)
    once = functools.partial(pl.BlockSpec, index_map=whole, pipeline_mode=pl.Buffered(1))
    across = lambda i: (0, i)
    down = lambda i: (i, 0)
    flops = 2 * units * (3 * rows * depth + 2 * own_rows * depth + 3 * rows * share)
    return pl.pallas_call(
        functools.partial(back_kernel, own_rows, len(pieces)),
        grid=(units // tile,),
        in_specs=[once((2 * CAP, depth)) for _ in pieces]
        + [
            pl.BlockSpec((depth, tile), across),
            pl.BlockSpec((depth, tile), across),
            pl.BlockSpec((tile, depth), down),
        ],
        out_specs=[
            pl.BlockSpec((share, tile), across),
            pl.BlockSpec((share, tile), across),
            pl.BlockSpec((tile, share), down),
            pl.BlockSpec((own_rows, depth), whole),
        ],
        out_shape=[
            jax.ShapeDtypeStruct((share, units), jnp.bfloat16),
            jax.ShapeDtypeStruct((share, units), jnp.bfloat16),
            jax.ShapeDtypeStruct((units, share), jnp.bfloat16),
            jax.ShapeDtypeStruct((own_rows, depth), jnp.bfloat16),
        ],
        scratch_shapes=[
            pltpu.VMEM((rows, depth), jnp.bfloat16),
            pltpu.VMEM((rows, depth), jnp.bfloat16),
            pltpu.VMEM((share, rows), jnp.bfloat16),
            pltpu.VMEM((rows, share), jnp.bfloat16),
            pltpu.VMEM((own_rows, depth), jnp.float32),
        ],
        compiler_params=pltpu.CompilerParams(vmem_limit_bytes=48 * 2**20),
        cost_estimate=pl.CostEstimate(
            flops=flops,
            bytes_accessed=6 * units * (depth + share) + 8 * rows * depth,
            transcendentals=rows * units,
        ),
    )(*pieces, gate_w, up_w, down_w)


def backward_plain(back_all, grad_all, gate_w, up_w, down_w, start):
    share = gate_w.shape[0] // lax.axis_size("dp")
    first = lax.axis_index("dp") * share
    back_cols = lax.dynamic_slice_in_dim(back_all, first, share, 1)
    grad_cols = lax.dynamic_slice_in_dim(grad_all, first, share, 1)
    pre_gate, pre_up = mul(back_all, gate_w), mul(back_all, up_w)
    hidden, grad_gate, grad_up = gates(pre_gate, pre_up, mul(grad_all, down_w, NT))
    own_rows = back_all.shape[0] // lax.axis_size("dp")
    own_gate = lax.dynamic_slice_in_dim(grad_gate, start, own_rows, 0)
    own_up = lax.dynamic_slice_in_dim(grad_up, start, own_rows, 0)
    return (
        mul(back_cols, grad_gate, TN).astype(jnp.bfloat16),
        mul(back_cols, grad_up, TN).astype(jnp.bfloat16),
        mul(hidden, grad_cols, TN).astype(jnp.bfloat16),
        (mul(own_gate, gate_w, NT) + mul(own_up, up_w, NT)).astype(jnp.bfloat16),
    )


def per_device(
    handoff,
    fwd_slot,
    fwd_weight,
    stashed,
    back_slot,
    back_weight,
    grad_handoff,
    w_gate,
    w_up,
    w_down,
):
    gate_w, up_w, down_w = (w_gate[0], w_up[0], w_down[0])
    fwd_ids, back_ids = fwd_slot[0], back_slot[0]
    fwd_ids_there = passed_along(fwd_slot, "section", -1)[0]
    back_ids_there = passed_along(back_slot, "section", 1)[0]
    arrived = passed_along(pack_rows(handoff[0], fwd_ids_there), "section", 1)
    returned = passed_along(pack_rows(grad_handoff[0], back_ids_there), "section", -1)
    stash_packed = pack_rows(stashed[0], back_ids)
    weights = pack_values(back_weight[0], back_ids)
    grad_packed = (weights[:, None] * returned.astype(jnp.float32)).astype(jnp.bfloat16)
    n_dp, n_et = lax.axis_size("dp"), lax.axis_size("et")

    if n_et == 2:
        block = jnp.concatenate([stash_packed, grad_packed], axis=0)
        arrived, block = lax.optimization_barrier((arrived, block))
        blocks = [passed_along(block, "dp", d) for d in range(1, n_dp)]
        fwd_rows, block = lax.optimization_barrier((gather_et(arrived), block))
        blocks = [block] + blocks
        pieces = [x for one in blocks for x in (one, passed_along(one, "et", 1))]
    else:
        fwd_rows = gather_et(arrived)
        pieces = [
            lax.all_gather(x, ("dp", "et"), axis=0, tiled=True) for x in (stash_packed, grad_packed)
        ]

    pre_gate = mul(fwd_rows, gate_w)
    pre_up = mul(fwd_rows, up_w)
    hidden = (pre_gate * jax.nn.sigmoid(pre_gate) * pre_up).astype(jnp.bfloat16)
    fwd_partial = mul(hidden, down_w).astype(jnp.bfloat16)
    sent, pieces = lax.optimization_barrier((sent_part(fwd_partial), pieces))
    own_sum = with_own(fwd_partial, sent)
    forward_out = (fwd_weight[0][:, None] * unpack_rows(own_sum, fwd_ids)).astype(jnp.bfloat16)

    tiles = [t for t in (384, 256, 128) if gate_w.shape[1] % t == 0]
    aligned = gate_w.shape[0] % (128 * n_dp) == 0
    if n_et == 2 and tiles and aligned and n_dp <= 8:
        grads = backward(pieces, gate_w, up_w, down_w, tiles[0])
    else:
        own = 0
        if n_et == 2:
            pieces = [jnp.concatenate([x[k : k + CAP] for x in pieces]) for k in (0, CAP)]
        else:
            own = lax.axis_index("dp") * n_et * CAP
        grads = backward_plain(*pieces, gate_w, up_w, down_w, own)
    gate_sum, up_sum, down_sum, partial = grads
    own_grad = with_own(partial, sent_part(partial))
    grad_rows = unpack_rows(own_grad, back_ids).astype(jnp.bfloat16)
    return (
        forward_out[None],
        grad_rows[None],
        gate_sum[None],
        up_sum[None],
        down_sum[None],
    )


def solution(mesh):
    rows3 = P("section", ("dp", "et"), None)
    rows2 = P("section", ("dp", "et"))
    columns = P("section", None, "et")
    return jax.shard_map(
        per_device,
        mesh=mesh,
        in_specs=(
            rows3, rows2, rows2, rows3, rows2, rows2, rows3,
            columns, columns, P("section", "et", None),
        ),
        out_specs=(
            rows3,
            rows3,
            P("section", "dp", "et"),
            P("section", "dp", "et"),
            P("section", "et", "dp"),
        ),
        check_vma=False,
    )
```

```python
import functools

import jax
import jax.numpy as jnp
from jax import lax
from jax.experimental import pallas as pl
from jax.experimental.pallas import tpu as pltpu
from jax.sharding import PartitionSpec as P

CAP = 32
NN = (((1,), (0,)), ((), ()))
NT = (((1,), (1,)), ((), ()))
TN = (((0,), (0,)), ((), ()))


def mul(a, b, dims=NN):
    return lax.dot_general(a, b, dims, preferred_element_type=jnp.float32)


def passed_along(block, axis, distance):
    n = lax.axis_size(axis)
    return lax.ppermute(block, axis, [((i - distance) % n, i) for i in range(n)])


def pack_rows(row_block, slot_ids):
    places = lax.broadcasted_iota(jnp.int32, (CAP, slot_ids.shape[0]), 0)
    picker = (places == slot_ids[None, :]).astype(jnp.bfloat16)
    return mul(picker, row_block).astype(jnp.bfloat16)


def pack_values(values, slot_ids):
    places = lax.broadcasted_iota(jnp.int32, (CAP, slot_ids.shape[0]), 0)
    return jnp.sum(jnp.where(places == slot_ids[None, :], values[None, :], 0.0), axis=1)


def unpack_rows(packed, slot_ids):
    places = lax.broadcasted_iota(jnp.int32, (slot_ids.shape[0], CAP), 1)
    picker = (places == slot_ids[:, None]).astype(jnp.float32)
    return jnp.dot(
        picker, packed, precision=lax.Precision.HIGHEST, preferred_element_type=jnp.float32
    )


def gather_et(rows):
    if lax.axis_size("et") == 2:
        return jnp.concatenate([rows, passed_along(rows, "et", 1)], axis=0)
    return lax.all_gather(rows, "et", axis=0, tiled=True)


def sent_part(partial):
    if lax.axis_size("et") == 2:
        return passed_along(partial[CAP:], "et", 1).astype(jnp.float32)
    return lax.psum_scatter(partial, "et", scatter_dimension=0, tiled=True).astype(jnp.float32)


def with_own(partial, sent):
    if lax.axis_size("et") == 2:
        return partial[:CAP].astype(jnp.float32) + sent
    return sent


def gates(pre_gate, pre_up, grad_hidden):
    sig = jax.nn.sigmoid(pre_gate)
    active = pre_gate * sig
    hidden = (active * pre_up).astype(jnp.bfloat16)
    grad_up = (grad_hidden * active).astype(jnp.bfloat16)
    grad_gate = (grad_hidden * pre_up * sig * (1.0 + pre_gate * (1.0 - sig))).astype(jnp.bfloat16)
    return hidden, grad_gate, grad_up


def back_kernel(own_rows, n_pieces, *refs):
    pieces, refs = refs[:n_pieces], refs[n_pieces:]
    gate_ref, up_ref, down_ref, gate_out, up_out, down_out, rows_out = refs[:7]
    back_ref, grad_ref, back_cols_t, grad_cols, total = refs[7:]
    step = pl.program_id(0)
    share = grad_cols.shape[1]

    @pl.when(step == 0)
    def _():
        for k, piece in enumerate(pieces):
            back_ref[k * CAP : (k + 1) * CAP] = piece[:CAP]
            grad_ref[k * CAP : (k + 1) * CAP] = piece[CAP:]
        columns = pl.ds(pl.multiple_of(lax.axis_index("dp") * share, 128), share)
        back_cols_t[...] = back_ref[:, columns].T
        grad_cols[...] = grad_ref[:, columns]

    pre_gate = mul(back_ref[...], gate_ref[...])
    pre_up = mul(back_ref[...], up_ref[...])
    grad_hidden = mul(grad_ref[...], down_ref[...], NT)
    hidden, grad_gate, grad_up = gates(pre_gate, pre_up, grad_hidden)
    gate_out[...] = mul(back_cols_t[...], grad_gate).astype(jnp.bfloat16)
    up_out[...] = mul(back_cols_t[...], grad_up).astype(jnp.bfloat16)
    down_out[...] = mul(hidden, grad_cols[...], TN).astype(jnp.bfloat16)
    term = mul(grad_gate[:own_rows], gate_ref[...], NT)
    term += mul(grad_up[:own_rows], up_ref[...], NT)

    @pl.when(step == 0)
    def _():
        total[...] = term

    @pl.when(step > 0)
    def _():
        total[...] += term

    @pl.when(step == pl.num_programs(0) - 1)
    def _():
        rows_out[...] = total[...].astype(jnp.bfloat16)


def backward(pieces, gate_w, up_w, down_w, tile):
    rows, depth = len(pieces) * CAP, gate_w.shape[0]
    share = depth // lax.axis_size("dp")
    units = gate_w.shape[1]
    own_rows = rows // lax.axis_size("dp")
    whole = lambda i: (0, 0)
    once = functools.partial(pl.BlockSpec, index_map=whole, pipeline_mode=pl.Buffered(1))
    across = lambda i: (0, i)
    down = lambda i: (i, 0)
    flops = 2 * units * (3 * rows * depth + 2 * own_rows * depth + 3 * rows * share)
    return pl.pallas_call(
        functools.partial(back_kernel, own_rows, len(pieces)),
        grid=(units // tile,),
        in_specs=[once((2 * CAP, depth)) for _ in pieces]
        + [
            pl.BlockSpec((depth, tile), across),
            pl.BlockSpec((depth, tile), across),
            pl.BlockSpec((tile, depth), down),
        ],
        out_specs=[
            pl.BlockSpec((share, tile), across),
            pl.BlockSpec((share, tile), across),
            pl.BlockSpec((tile, share), down),
            pl.BlockSpec((own_rows, depth), whole),
        ],
        out_shape=[
            jax.ShapeDtypeStruct((share, units), jnp.bfloat16),
            jax.ShapeDtypeStruct((share, units), jnp.bfloat16),
            jax.ShapeDtypeStruct((units, share), jnp.bfloat16),
            jax.ShapeDtypeStruct((own_rows, depth), jnp.bfloat16),
        ],
        scratch_shapes=[
            pltpu.VMEM((rows, depth), jnp.bfloat16),
            pltpu.VMEM((rows, depth), jnp.bfloat16),
            pltpu.VMEM((share, rows), jnp.bfloat16),
            pltpu.VMEM((rows, share), jnp.bfloat16),
            pltpu.VMEM((own_rows, depth), jnp.float32),
        ],
        compiler_params=pltpu.CompilerParams(vmem_limit_bytes=48 * 2**20),
        cost_estimate=pl.CostEstimate(
            flops=flops,
            bytes_accessed=6 * units * (depth + share) + 8 * rows * depth,
            transcendentals=rows * units,
        ),
    )(*pieces, gate_w, up_w, down_w)


def backward_plain(back_all, grad_all, gate_w, up_w, down_w, start):
    share = gate_w.shape[0] // lax.axis_size("dp")
    first = lax.axis_index("dp") * share
    back_cols = lax.dynamic_slice_in_dim(back_all, first, share, 1)
    grad_cols = lax.dynamic_slice_in_dim(grad_all, first, share, 1)
    pre_gate, pre_up = mul(back_all, gate_w), mul(back_all, up_w)
    hidden, grad_gate, grad_up = gates(pre_gate, pre_up, mul(grad_all, down_w, NT))
    own_rows = back_all.shape[0] // lax.axis_size("dp")
    own_gate = lax.dynamic_slice_in_dim(grad_gate, start, own_rows, 0)
    own_up = lax.dynamic_slice_in_dim(grad_up, start, own_rows, 0)
    return (
        mul(back_cols, grad_gate, TN).astype(jnp.bfloat16),
        mul(back_cols, grad_up, TN).astype(jnp.bfloat16),
        mul(hidden, grad_cols, TN).astype(jnp.bfloat16),
        (mul(own_gate, gate_w, NT) + mul(own_up, up_w, NT)).astype(jnp.bfloat16),
    )


def per_device(
    handoff,
    fwd_slot,
    fwd_weight,
    stashed,
    back_slot,
    back_weight,
    grad_handoff,
    w_gate,
    w_up,
    w_down,
):
    gate_w, up_w, down_w = (w_gate[0], w_up[0], w_down[0])
    fwd_ids, back_ids = fwd_slot[0], back_slot[0]
    fwd_ids_there = passed_along(fwd_slot, "section", -1)[0]
    back_ids_there = passed_along(back_slot, "section", 1)[0]
    arrived = passed_along(pack_rows(handoff[0], fwd_ids_there), "section", 1)
    returned = passed_along(pack_rows(grad_handoff[0], back_ids_there), "section", -1)
    stash_packed = pack_rows(stashed[0], back_ids)
    weights = pack_values(back_weight[0], back_ids)
    grad_packed = (weights[:, None] * returned.astype(jnp.float32)).astype(jnp.bfloat16)
    n_dp, n_et = lax.axis_size("dp"), lax.axis_size("et")

    if n_et == 2:
        block = jnp.concatenate([stash_packed, grad_packed], axis=0)
        arrived, block = lax.optimization_barrier((arrived, block))
        blocks = [passed_along(block, "dp", d) for d in range(1, n_dp)]
        fwd_rows, block = lax.optimization_barrier((gather_et(arrived), block))
    else:
        fwd_rows = gather_et(arrived)
        pieces = [
            lax.all_gather(x, ("dp", "et"), axis=0, tiled=True) for x in (stash_packed, grad_packed)
        ]

    pre_gate = mul(fwd_rows, gate_w)
    if n_et == 2:
        pre_gate, last = lax.optimization_barrier((pre_gate, blocks[-1]))
    pre_up = mul(fwd_rows, up_w)
    hidden = (pre_gate * jax.nn.sigmoid(pre_gate) * pre_up).astype(jnp.bfloat16)
    fwd_partial = mul(hidden, down_w).astype(jnp.bfloat16)
    if n_et == 2:
        swapped = passed_along(last, "et", 1)
        fwd_partial, early, swapped = lax.optimization_barrier((fwd_partial, blocks[:-1], swapped))
        pieces = [x for one in [block] + early for x in (one, passed_along(one, "et", 1))]
        pieces += [last, swapped]
    sent, pieces = lax.optimization_barrier((sent_part(fwd_partial), pieces))
    own_sum = with_own(fwd_partial, sent)
    forward_out = (fwd_weight[0][:, None] * unpack_rows(own_sum, fwd_ids)).astype(jnp.bfloat16)

    tiles = [t for t in (384, 256, 128) if gate_w.shape[1] % t == 0]
    aligned = gate_w.shape[0] % (128 * n_dp) == 0
    if n_et == 2 and tiles and aligned and n_dp <= 8:
        grads = backward(pieces, gate_w, up_w, down_w, tiles[0])
    else:
        own = 0
        if n_et == 2:
            pieces = [jnp.concatenate([x[k : k + CAP] for x in pieces]) for k in (0, CAP)]
        else:
            own = lax.axis_index("dp") * n_et * CAP
        grads = backward_plain(*pieces, gate_w, up_w, down_w, own)
    gate_sum, up_sum, down_sum, partial = grads
    own_grad = with_own(partial, sent_part(partial))
    grad_rows = unpack_rows(own_grad, back_ids).astype(jnp.bfloat16)
    return (
        forward_out[None],
        grad_rows[None],
        gate_sum[None],
        up_sum[None],
        down_sum[None],
    )


def solution(mesh):
    rows3 = P("section", ("dp", "et"), None)
    rows2 = P("section", ("dp", "et"))
    columns = P("section", None, "et")
    return jax.shard_map(
        per_device,
        mesh=mesh,
        in_specs=(
            rows3, rows2, rows2, rows3, rows2, rows2, rows3,
            columns, columns, P("section", "et", None),
        ),
        out_specs=(
            rows3,
            rows3,
            P("section", "dp", "et"),
            P("section", "dp", "et"),
            P("section", "et", "dp"),
        ),
        check_vma=False,
    )
```
